768 devices in a mesh: dp: 32 (over y, z_hi, core), mp: 24 (over z_lo, x).
Axes of the slice: x: 4, y: 8, z: 12 (z_hi: 2, z_lo: 6; z = z_hi * 6 + z_lo), core: 2. Of those that a mesh axis runs over, the one named last changes fastest.
Arguments:
- patches: bfloat16 [4160, 1152, 256], P('dp', 'mp'), may hold values from -6 to 6
- picked: int32 [416], replicated, may hold values from 0 to 4159, as said below
- text_embed: bfloat16 [416, 1152], P('dp'), may hold values from -400 to 400
- weight_in: bfloat16 [1152, 2304], P(None, 'mp'), may hold values from -0.1875 to 0.1875
- weight_out: bfloat16 [2304, 1152], P('mp'), may hold values from -0.125 to 0.125
- logit_scale: float32 [1], replicated, may hold values from 3 to 8
- logit_bias: float32 [1], replicated, may hold values from -4 to -1
Outputs:
- embed_grad: float32 [416, 1152], P('dp')
The draws below stay inside these ranges and needn't reach their ends.
Inputs may be any that keep to these rules, and one draw needn't show every extreme that they name: `picked`: entries are distinct super-batch indices; entries d*13 to (d+1)*13 - 1 belong to learner d; of them at most 2 lie in one source block of 130 consecutive indices, and exactly 2 do for some source in every learner's list.
All inputs are finite; a program needn't handle non-finite values.
Results may differ from the reference program's by a relative error of at most 0.00075.
Values may be sent and summed in bfloat16 or wider, within the bound.
A program may use at most 64 MiB of HBM per device.

```python
import math
import jax
import jax.numpy as jnp
from jax import lax

D = 1152
FF = 2304
P_SIZE = 256
CAP = 2
IMG_DEV = 13
SUP_DEV = 130
SUPER = 4160
BATCH = 416


def draw_picked(key, part):
    key = jax.random.fold_in(key, 11)
    key_pop, key_raw, key_force, key_order, key_shift = jax.random.split(key, 5)
    learners = BATCH // IMG_DEV
    position_table = learners * CAP
    position_index = jnp.arange(position_table, dtype=jnp.int32)
    position_provider = position_index // CAP
    frequent_choice = jax.random.randint(key_pop, (learners,), 0, 4)
    unadjusted_rating = jax.random.randint(key_raw, (learners, position_table), 0, 4096)
    mandatory_pick = jax.random.randint(key_force, (learners,), 0, learners)
    extra_reward = (position_provider[None, :] == mandatory_pick[:, None]).astype(jnp.int32) * 100000
    selection_rating = (unadjusted_rating + frequent_choice[position_provider][None, :] * 2048 + extra_reward) * position_table + position_index[None, :]
    top_vals, chosen = lax.top_k(selection_rating, IMG_DEV)
    source = (chosen // CAP).astype(jnp.int32)
    order_key = jax.random.randint(key_order, (learners, IMG_DEV), 0, 4096) * IMG_DEV + jnp.arange(IMG_DEV, dtype=jnp.int32)[None, :]
    reorder = jnp.argsort(order_key, axis=1, stable=True)
    source = jnp.take_along_axis(source, reorder, axis=1)
    flat = source.reshape(-1)
    positions = jnp.arange(flat.shape[0], dtype=jnp.int32)
    same_src = flat[:, None] == flat[None, :]
    earlier = positions[:, None] > positions[None, :]
    rank_in = jnp.sum((same_src & earlier).astype(jnp.int32), axis=1)
    shifts = jax.random.randint(key_shift, (learners,), 0, SUP_DEV)
    local_idx = (rank_in + shifts[flat]) % SUP_DEV
    return (flat * SUP_DEV + local_idx).astype(jnp.int32)


def draw_text_embed(key, part):
    key = jax.random.fold_in(key, 5)
    key_rows, key_cols, key_base = jax.random.split(key, 3)
    row_scale = jnp.exp(jax.random.uniform(key_rows, (BATCH, 1), jnp.float32) * math.log(10.0))
    col_scale = jnp.exp(jax.random.uniform(key_cols, (1, D), jnp.float32) * math.log(10.0))
    base = jnp.clip(jax.random.normal(key_base, (BATCH, D), jnp.float32), -4.0, 4.0)
    return (base * row_scale * col_scale).astype(jnp.bfloat16)


def levels(stream_key, dims, shards, smallest, top_value):
    gain, own = 1.0, jax.random.fold_in(stream_key, 6)
    for position, blocks in shards:
        steps = jnp.exp(jax.random.uniform(jax.random.fold_in(own, position), (blocks,), jnp.float32, smallest / len(shards), top_value / len(shards)))
        gain = gain * jnp.repeat(steps, dims[position] // blocks).reshape([-1 if axis == position else 1 for axis in range(len(dims))])
    return gain


def gaussian(key, extent, width, bound, shards=(), kind=jnp.bfloat16):
    values = jax.random.normal(key, extent, jnp.float32) * width
    if len(shards) > 0:
        values = levels(key, extent, shards, -0.22, 0.18) * values
    return jnp.clip(values, min=-bound, max=bound).astype(kind)


def setup_inputs(seed: int = 0) -> dict:
    arg_keys = jax.random.split(jax.random.key(seed), 8)
    patches = gaussian(arg_keys[0], (SUPER, D, P_SIZE), 1.0, 6.0, ((0, 32), (1, 24)))
    picked = draw_picked(jax.random.fold_in(arg_keys[7], 71), 0)
    text_embed = draw_text_embed(jax.random.fold_in(arg_keys[7], 71), 0)
    weight_in = gaussian(arg_keys[3], (D, FF), D ** -0.5, 0.1875, ((1, 24),))
    weight_out = gaussian(arg_keys[4], (FF, D), FF ** -0.5, 0.125, ((0, 24),))
    logit_scale = jnp.clip(jax.random.uniform(arg_keys[5], (1,), jnp.float32, 3.0, 8.0), 3.0, 8.0)
    logit_bias = jnp.clip(jax.random.uniform(arg_keys[6], (1,), jnp.float32, -4.0, -1.0), -4.0, -1.0)
    return {"patches": patches, "picked": picked, "text_embed": text_embed, "weight_in": weight_in, "weight_out": weight_out, "logit_scale": logit_scale, "logit_bias": logit_bias}


layer_eps = 1e-06

def reference(patches, picked, text_embed, weight_in, weight_out, logit_scale, logit_bias):

    def embed_one(index):
        chosen = jnp.transpose(patches[index])
        values = chosen.astype(jnp.float32)
        center = lax.optimization_barrier(jnp.mean(values, axis=-1, keepdims=True))
        spread = lax.optimization_barrier(jnp.mean((values - center) ** 2, axis=-1, keepdims=True))
        normed = ((values - center) * lax.rsqrt(spread + layer_eps)).astype(jnp.bfloat16)
        hidden = jax.nn.gelu(jnp.dot(normed, weight_in, preferred_element_type=jnp.float32), approximate=True)
        pooled = lax.optimization_barrier(jnp.mean(hidden, axis=0)).astype(jnp.bfloat16)
        branch = jnp.dot(pooled, weight_out, preferred_element_type=jnp.float32)
        return lax.optimization_barrier(jnp.mean(values, axis=0)) + branch
    embed = lax.map(embed_one, picked)
    length = jnp.sqrt(lax.optimization_barrier(jnp.sum(embed * embed, axis=-1, keepdims=True)) + layer_eps)
    unit = embed / length
    text_vals = text_embed.astype(jnp.float32)
    text_unit = text_vals / jnp.sqrt(lax.optimization_barrier(jnp.sum(text_vals * text_vals, axis=-1, keepdims=True)) + layer_eps)
    scale = logit_scale[0]
    logits = scale * jnp.dot(unit, text_unit.T, precision=lax.Precision.HIGHEST) + logit_bias[0]
    count = embed.shape[0]
    label = jnp.where(jnp.arange(count)[:, None] == jnp.arange(count)[None, :], 1.0, -1.0).astype(jnp.float32)
    slope = -label * jax.nn.sigmoid(-label * logits)
    unit_grad = scale * jnp.dot(slope, text_unit, precision=lax.Precision.HIGHEST)
    along = lax.optimization_barrier(jnp.sum(unit * unit_grad, axis=-1, keepdims=True))
    return (unit_grad - unit * along) / length
```

```python
import jax
import jax.numpy as jnp
from jax import lax
from jax.experimental import pallas as pl
from jax.experimental.pallas import tpu as pltpu
from jax.sharding import PartitionSpec as P

MESH = pl.DeviceIdType.MESH
F32, BF16 = jnp.float32, jnp.bfloat16
EPS = 1e-06
NY, NH, NC, NQ, NX = 8, 2, 2, 6, 4
NZ = NH * NQ
NS = NY * NC
IMG = 13
SUP = 130
FEAT, NP = 48, 256
D, HID = 1152, 576
ROWS, LANES = 16, 128
NF, NPC = FEAT // ROWS, NP // LANES
CH = NF * NPC
AHEAD = 3
EXTRA = 2
NT = (((1,), (1,)), ((), ()))


def split3(v):
    hi = v.astype(BF16)
    rest = v - hi.astype(F32)
    mid = rest.astype(BF16)
    lo = (rest - mid.astype(F32)).astype(BF16)
    return jnp.concatenate([hi, mid, lo], axis=0)


def sum3(v):
    n = v.shape[0] // 3
    return (v[2 * n :] + v[n : 2 * n]) + v[:n]


def row_ones(r, width, value, dtype):
    rows = lax.broadcasted_iota(jnp.int32, (8, width), 0)
    return jnp.where(rows == r, F32(value), F32(0.0)).astype(dtype)


def kernel(*refs):
    (patches, send_idx, comp_idx, half_idx, text, w_in, w_out, scale_ref, bias_ref, out) = refs[:10]
    refs = refs[10:]
    pv, wv, ys, zs, xb, wb, tb, normed, acc, pooled, mean_rows, f1, f2, itl = refs[:14]
    yr = refs[14 : 14 + CH]
    zr = refs[14 + CH : 14 + 2 * CH]
    (lsem, ysend, yrecv, zsend, zrecv, zxsend, zxrecv, xsend, xrecv, wsend, wrecv, dsend, drecv,
     tsend, trecv, f1send, f1recv, f2send, f2recv) = refs[14 + 2 * CH :]

    dp = lax.axis_index("dp")
    mp = lax.axis_index("mp")
    y, h, c = dp // 4, (dp // 2) % 2, dp % 2
    q, x = mp // NX, mp % NX
    z = h * NQ + q
    me = y * NC + c

    def ydev(s):
        return (((s // 2) * 2 + h) * 2 + s % 2, mp)

    def zdev(t):
        return ((y * 2 + t // NQ) * 2 + c, (t % NQ) * NX + x)

    def xdev(k):
        return (dp, q * NX + k)

    def core_dev():
        return (y * 4 + h * 2 + 1 - c, mp)

    def remote(src, dst, ssem, rsem, dev):
        return pltpu.make_async_remote_copy(
            src_ref=src, dst_ref=dst, send_sem=ssem, recv_sem=rsem, device_id=dev, device_id_type=MESH)

    def wait(ref, sem):
        pltpu.make_async_copy(ref, ref, sem).wait()

    load_p = pltpu.make_async_copy(patches, pv, lsem.at[0])
    load_p.start()
    load_i = pltpu.make_async_copy(w_in, wv, lsem.at[1])
    load_i.start()
    load_o = pltpu.make_async_copy(w_out, wb.at[1, q], lsem.at[2])
    load_o.start()

    barrier = pltpu.get_barrier_semaphore()

    def greet(dev):
        pl.semaphore_signal(barrier, inc=1, device_id=dev, device_id_type=MESH)

    @pl.loop(1, NS)
    def _(o):
        greet(ydev((me + o) % NS))

    @pl.loop(1, NZ)
    def _(o):
        greet(zdev((z + o) % NZ))

    @pl.loop(1, NX)
    def _(o):
        greet(xdev((x + o) % NX))

    @pl.when(y // 2 == x)
    def _():
        tb[c, h, y] = jnp.concatenate([text[...].astype(F32), jnp.zeros((ROWS - IMG, D), F32)], axis=0).astype(BF16)

    def gather(k):
        pc, fc = k // NF, k % NF

        @pl.loop(0, NS * 4, unroll=8)
        def _(s):
            image = pv[send_idx[s], fc * ROWS : (fc + 1) * ROWS, pc * LANES : (pc + 1) * LANES]
            ys[k, s // 4, s % 4] = image

        yr[k][pl.ds(me * 4, 4)] = ys[k, me]

    def start_y(k):
        @pl.loop(1, NS)
        def _(o):
            s = (me + o) % NS
            remote(ys.at[k, s], yr[k].at[pl.ds(me * 4, 4)], ysend.at[k], yrecv.at[k], ydev(s)).start()

    load_p.wait()
    gather(0)
    pl.semaphore_wait(barrier, NS - 1 + NZ - 1 + NX - 1)
    start_y(0)
    load_i.wait()
    load_o.wait()
    rows = lax.broadcasted_iota(jnp.int32, (96, 96), 0)
    cols = lax.broadcasted_iota(jnp.int32, (96, 96), 1)
    eye = jnp.where(rows == cols, F32(1.0), F32(0.0)).astype(BF16)
    wb[0, q] = lax.dot_general(eye, wv[...], NT, preferred_element_type=F32).astype(BF16)

    up, down = (z + 1) % NZ, (z + NZ - 1) % NZ

    def qq(k):
        return (q + k + NQ) % NQ

    def w_piece(rnd, way):
        k = qq(-rnd if way == 0 else rnd)
        if rnd == 2:
            return wb.at[c, k, pl.ds(0 if way == 0 else 48, 48)]
        return wb.at[c, k]

    def w_copy(rnd, way):
        piece = w_piece(rnd, way)
        return remote(piece, piece, wsend.at[rnd, way], wrecv.at[rnd, way], zdev(up if way == 0 else down))

    def w_start(rnd):
        w_copy(rnd, 0).start()
        w_copy(rnd, 1).start()

    def w_wait(rnd):
        w_copy(rnd, 0).wait_recv()
        w_copy(rnd, 1).wait_recv()

    def d_copy(j):
        k = (qq(-1), qq(1), qq(-2), qq(2), qq(3))[j]
        return remote(wb.at[c, k], wb.at[c, k], dsend.at[j], drecv.at[j], core_dev())

    w_start(0)
    gather(1)
    start_y(1)

    @pl.when(y // 2 == x)
    def _():
        @pl.loop(1, NY)
        def _(o):
            to = (y + o) % NY
            remote(tb.at[c, h, y], tb.at[c, h, y], tsend.at[0], trecv.at[y % 2], ((to * 2 + h) * 2 + c, mp)).start()

    gather(2)
    start_y(2)

    def t_mirror():
        piece = tb.at[c, h, pl.ds(2 * x, 2)]
        return remote(piece, piece, tsend.at[1], trecv.at[2], zdev(NZ - 1 - z))

    def t_gather(k):
        piece = tb.at[c, :, pl.ds(2 * x, 2)]
        return remote(piece, piece, tsend.at[2], trecv.at[3 + x], xdev(k))

    def t_core():
        return remote(tb.at[c], tb.at[c], tsend.at[3], trecv.at[7], core_dev())

    def compact(k):
        @pl.loop(0, NZ * 3, unroll=6)
        def _(g):
            zs[k, g // 3, g % 3] = yr[k][comp_idx[g]]

        zr[k][z] = zs[k, z]

    def start_z(k):
        @pl.loop(1, NZ)
        def _(o):
            t = (z + o) % NZ
            remote(zs.at[k, t, pl.ds(0, 2)], zr[k].at[z, pl.ds(0, 2)], zsend.at[k], zrecv.at[k], zdev(t)).start()

        for e in range(NH):
            t = e * NQ + EXTRA

            @pl.when(z != t)
            def _():
                remote(zs.at[k, t, pl.ds(2, 1)], zr[k].at[z, pl.ds(2, 1)], zxsend.at[k, e], zxrecv.at[k], zdev(t)).start()

    extra = q == EXTRA

    def wait_z(k):
        wait(zr[k].at[pl.ds(0, NZ - 1), pl.ds(0, 2)], zrecv.at[k])

        @pl.when(extra)
        def _():
            wait(zr[k].at[pl.ds(0, NZ - 1), pl.ds(2, 1)], zxrecv.at[k])

    def select(k):
        pc, fc = k // NF, k % NF

        @pl.loop(0, NQ)
        def _(s):
            for r in range(2):
                xb[pc, r, s, x, fc] = zr[k][half_idx[r] + s, r]

        @pl.when(extra)
        def _():
            @pl.loop(0, NQ)
            def _(s):
                xb[pc, 2, s, x, fc] = zr[k][half_idx[2] + s, 2]

    def x_piece(k, r0, n, owner):
        return xb.at[k // NF, pl.ds(r0, n), :, owner, k % NF]

    def x_copy(k, r0, n, owner, to):
        piece = x_piece(k, r0, n, owner)
        i = 0 if r0 == 0 else 1
        return remote(piece, piece, xsend.at[k, i, to], xrecv.at[k, i, owner], xdev(to))

    def start_x(k):
        @pl.loop(1, NX)
        def _(o):
            x_copy(k, 0, 2, x, (x + o) % NX).start()

        @pl.when(extra)
        def _():
            @pl.loop(1, NX)
            def _(o):
                x_copy(k, 2, 1, x, (x + o) % NX).start()

    def wait_x(k):
        @pl.loop(1, NX)
        def _(o):
            owner = (x + o) % NX
            wait(x_piece(k, 0, 2, owner), xrecv.at[k, 0, owner])

        @pl.when(extra)
        def _():
            @pl.loop(1, NX)
            def _(o):
                owner = (x + o) % NX
                wait(x_piece(k, 2, 1, owner), xrecv.at[k, 1, owner])

    def normalize(pc, r):
        flat = xb[pc, r].reshape(D, LANES)
        values = flat.astype(F32)
        center = jnp.sum(values, axis=0, keepdims=True) * F32(1.0 / D)
        values = values - center
        spread = jnp.sum(values * values, axis=0, keepdims=True) * F32(1.0 / D)
        mean = lax.dot_general(row_ones(r, LANES, 1.0 / (NP * NX), BF16), flat, NT, preferred_element_type=F32)
        mean_rows[...] += mean
        return (values * lax.rsqrt(spread + F32(EPS))).astype(BF16)

    def hidden(pc, lanes, first):
        weights = wb[0].reshape(HID, D)
        value = jnp.dot(weights, normed[:, lanes], preferred_element_type=F32)
        value = jax.nn.gelu(value, approximate=True)
        if pc == 0:
            acc[:, lanes] = value
        else:
            acc[:, lanes] += value

    def compute(pc):
        normed[:, 0:LANES] = normalize(pc, 0)
        normed[:, LANES : 2 * LANES] = normalize(pc, 1)
        hidden(pc, slice(0, 2 * LANES), 0)

        @pl.when(extra)
        def _():
            normed[:, 2 * LANES :] = normalize(pc, 2)
            hidden(pc, slice(2 * LANES, 3 * LANES), 2)

    def pool(r):
        total = acc[:, r * LANES : (r + 1) * LANES]
        pooled[...] += lax.dot_general(
            row_ones(r, LANES, 1.0 / NP, F32), total, NT, precision=lax.Precision.HIGHEST, preferred_element_type=F32)

    mean_rows[...] = jnp.zeros((8, D), F32)
    pooled[...] = jnp.zeros((8, HID), F32)

    for k in range(CH):
        wait(yr[k].at[pl.ds(0, (NS - 1) * 4)], yrecv.at[k])
        compact(k)
        start_z(k)
        if k + AHEAD < CH:
            gather(k + AHEAD)
            start_y(k + AHEAD)
        if k == 0:
            w_wait(0)
            w_start(1)
            d_copy(0).start()
            d_copy(1).start()
            for j in range(2):

                @pl.when(2 * x + j != y)
                def _():
                    wait(tb.at[c, h, 2 * x + j], trecv.at[j])

            t_mirror().start()
        elif k == 1:
            w_wait(1)
            w_start(2)
            d_copy(2).start()
            d_copy(3).start()
            t_mirror().wait_recv()

            @pl.loop(1, NX)
            def _(o):
                t_gather((x + o) % NX).start()
        elif k == 2:
            w_wait(2)
            d_copy(4).start()

            @pl.loop(1, NX)
            def _(o):
                owner = (x + o) % NX
                wait(tb.at[c, :, pl.ds(2 * owner, 2)], trecv.at[3 + owner])

            t_core().start()
        if k >= 1:
            wait_z(k - 1)
            select(k - 1)
            start_x(k - 1)
        if k == 4:
            for j in range(5):
                kk = (qq(-1), qq(1), qq(-2), qq(2), qq(3))[j]
                wait(wb.at[1 - c, kk], drecv.at[j])
            for j in range(NF):
                wait_x(j)
            compute(0)
    wait(tb.at[1 - c], trecv.at[7])
    squares = tb[...].reshape(NS * NH * ROWS, D).astype(F32)
    squares = squares * squares
    hi = squares.astype(BF16)
    lo = (squares - hi.astype(F32)).astype(BF16)
    ones = jnp.ones((8, D), BF16)
    total = lax.dot_general(ones, lo, NT, preferred_element_type=F32)
    total = total + lax.dot_general(ones, hi, NT, preferred_element_type=F32)
    itl[...] = 1.0 / jnp.sqrt(total + F32(EPS))

    wait_z(CH - 1)
    select(CH - 1)
    start_x(CH - 1)
    for j in range(NF, CH):
        wait_x(j)
    compute(1)
    pool(0)
    pool(1)

    @pl.when(extra)
    def _():
        pool(2)

    embed = jnp.dot(pooled[...].astype(BF16), wb[1].reshape(HID, D), preferred_element_type=F32)
    f1[x] = embed + mean_rows[...]

    def f1_copy(owner, to):
        return remote(f1.at[owner], f1.at[owner], f1send.at[to], f1recv.at[owner], xdev(to))

    @pl.loop(1, NX)
    def _(o):
        f1_copy(x, (x + o) % NX).start()

    @pl.loop(1, NX)
    def _(o):
        owner = (x + o) % NX
        wait(f1.at[owner], f1recv.at[owner])

    f2[q] = (f1[0] + f1[1]) + (f1[2] + f1[3])

    def f2_copy(owner, to):
        return remote(f2.at[owner], f2.at[owner], f2send.at[to], f2recv.at[owner], (dp, to * NX + x))

    @pl.loop(1, NQ)
    def _(o):
        f2_copy(q, (q + o) % NQ).start()

    @pl.loop(1, NQ)
    def _(o):
        owner = (q + o) % NQ
        wait(f2.at[owner], f2recv.at[owner])

    plane = f2[...]
    embed = jnp.concatenate(
        [plane[k, 0:2] for k in range(NQ)] + [plane[EXTRA, 2:3], jnp.zeros((ROWS - IMG, D), F32)], axis=0)
    length = jnp.sqrt(jnp.sum(embed * embed, axis=1, keepdims=True) + F32(EPS))
    unit = embed / length
    scale = scale_ref[0]
    table = tb[...].reshape(NS * NH * ROWS, D)
    dots = sum3(lax.dot_general(split3(unit), table, NT, preferred_element_type=F32))
    inverse = itl[0:1, :]
    logits = scale * (dots * inverse) + bias_ref[0]
    row = lax.broadcasted_iota(jnp.int32, logits.shape, 0)
    col = lax.broadcasted_iota(jnp.int32, logits.shape, 1)
    label = jnp.where(col == ((c * NH + h) * NY + y) * ROWS + row, F32(1.0), F32(-1.0))
    slope = -label * jax.nn.sigmoid(-label * logits)
    summed = sum3(jnp.dot(split3(slope * inverse), table, preferred_element_type=F32))
    unit_grad = scale * summed
    along = jnp.sum(unit * unit_grad, axis=1, keepdims=True)
    out[...] = ((unit_grad - unit * along) / length)[0:IMG]

    for k in range(CH):
        wait(yr[k].at[pl.ds(0, (NS - 1) * 4)], ysend.at[k])
        wait(zs.at[k, pl.ds(0, NZ - 1), pl.ds(0, 2)], zsend.at[k])
        for e in range(NH):
            t = e * NQ + EXTRA

            @pl.when(z != t)
            def _():
                wait(zs.at[k, t, pl.ds(2, 1)], zxsend.at[k, e])

        @pl.loop(1, NX)
        def _(o):
            x_copy(k, 0, 2, x, (x + o) % NX).wait_send()

        @pl.when(extra)
        def _():
            @pl.loop(1, NX)
            def _(o):
                x_copy(k, 2, 1, x, (x + o) % NX).wait_send()

    for rnd in range(3):
        w_copy(rnd, 0).wait_send()
        w_copy(rnd, 1).wait_send()
    for j in range(5):
        d_copy(j).wait_send()

    @pl.when(y // 2 == x)
    def _():
        wait(tb.at[c, h, pl.ds(0, NY - 1)], tsend.at[0])

    t_mirror().wait_send()
    wait(tb.at[pl.ds(0, 1), :, pl.ds(0, 6)], tsend.at[2])
    t_core().wait_send()

    @pl.loop(1, NX)
    def _(o):
        f1_copy(x, (x + o) % NX).wait_send()

    @pl.loop(1, NQ)
    def _(o):
        f2_copy(q, (q + o) % NQ).wait_send()


def body(patches, picked, text_embed, weight_in, weight_out, logit_scale, logit_bias):
    dp = lax.axis_index("dp")
    y, h, c = dp // 4, (dp // 2) % 2, dp % 2
    q = lax.axis_index("mp") // NX
    i32 = jnp.int32
    lists = picked.reshape(32, IMG)
    source = lists // SUP
    local = lists - source * SUP
    order = jnp.arange(IMG, dtype=i32)
    same = (source[:, :, None] == source[:, None, :]) & (order[:, None] > order[None, :])[None]
    slot = jnp.sum(same.astype(i32), axis=2)
    mine = source == dp
    send_idx = jnp.stack([jnp.sum(jnp.where(mine & (slot == k), local, 0), axis=1) for k in range(2)], axis=1)
    send_idx = send_idx.reshape(NY, NH, NC, 2).transpose(0, 2, 1, 3).reshape(NS * 4)

    def pair(a):
        return jnp.take(a.reshape(NY, NH, NC, IMG), y, axis=0)[:, c]

    src, slots = pair(source), pair(slot)
    src_half = (src // 2) % 2
    flat = ((src // 4) * 2 + src % 2) * 4 + jnp.arange(NH, dtype=i32)[:, None] * 2 + slots
    flat = jnp.where(src_half == h, flat, 0)
    last = jnp.broadcast_to(flat[:, None, IMG - 1 :], (NH, NQ, 1))
    comp_idx = jnp.concatenate([flat[:, : IMG - 1].reshape(NH, NQ, 2), last], axis=2).reshape(NZ * 3)
    own = jnp.take(src_half, h, axis=0)
    half_idx = NQ * jnp.concatenate([lax.dynamic_slice(own, (2 * q,), (2,)), own[IMG - 1 :]])

    smem = pl.BlockSpec(memory_space=pltpu.SMEM)
    hbm = pl.BlockSpec(memory_space=pl.ANY)
    vmem = pl.BlockSpec(memory_space=pltpu.VMEM)
    dma = pltpu.SemaphoreType.DMA
    return pl.pallas_call(
        kernel,
        out_shape=jax.ShapeDtypeStruct((IMG, D), F32),
        in_specs=[hbm, smem, smem, smem, vmem, hbm, hbm, smem, smem],
        out_specs=vmem,
        scratch_shapes=[
            pltpu.VMEM((SUP, FEAT, NP), BF16),
            pltpu.VMEM((D, 96), BF16),
            pltpu.VMEM((CH, NS, 4, ROWS, LANES), BF16),
            pltpu.VMEM((CH, NZ, 3, ROWS, LANES), BF16),
            pltpu.VMEM((NPC, 3, NQ, NX, NF, ROWS, LANES), BF16),
            pltpu.VMEM((2, NQ, 96, D), BF16),
            pltpu.VMEM((NC, NH, NY, ROWS, D), BF16),
            pltpu.VMEM((D, 3 * LANES), BF16),
            pltpu.VMEM((HID, 3 * LANES), F32),
            pltpu.VMEM((8, HID), F32),
            pltpu.VMEM((8, D), F32),
            pltpu.VMEM((NX, 8, D), F32),
            pltpu.VMEM((NQ, 8, D), F32),
            pltpu.VMEM((8, NS * NH * ROWS), F32),
        ]
        + [pltpu.VMEM((NS * 4, ROWS, LANES), BF16)] * CH
        + [pltpu.VMEM((NZ, 3, ROWS, LANES), BF16)] * CH
        + [
            dma((3,)), dma((CH,)), dma((CH,)), dma((CH,)), dma((CH,)), dma((CH, NH)), dma((CH,)),
            dma((CH, 2, NX)), dma((CH, 2, NX)), dma((3, 2)), dma((3, 2)), dma((5,)), dma((5,)),
            dma((4,)), dma((8,)), dma((NX,)), dma((NX,)), dma((NQ,)), dma((NQ,)),
        ],
        compiler_params=pltpu.CompilerParams(
            collective_id=0, has_side_effects=True, vmem_limit_bytes=50 * 1024 * 1024),
        cost_estimate=pl.CostEstimate(flops=2_000_000_000, bytes_accessed=5_000_000, transcendentals=1_000_000),
    )(patches, send_idx.astype(i32), comp_idx.astype(i32), half_idx.astype(i32), text_embed, weight_in, weight_out,
      logit_scale, logit_bias)


def solution(mesh):
    in_specs = (P("dp", "mp", None), P(), P("dp", None), P(None, "mp"), P("mp", None), P(), P())
    return jax.shard_map(body, mesh=mesh, in_specs=in_specs, out_specs=P("dp", None), check_vma=False)
```

```python
import jax
import jax.numpy as jnp
from jax import lax
from jax.experimental import pallas as pl
from jax.experimental.pallas import tpu as pltpu
from jax.sharding import PartitionSpec as P

MESH = pl.DeviceIdType.MESH
F32, BF16 = jnp.float32, jnp.bfloat16
EPS = 1e-06
NY, NH, NC, NQ, NX = 8, 2, 2, 6, 4
NZ = NH * NQ
NS = NY * NC
IMG = 13
SUP = 130
FEAT, NP = 48, 256
D, HID = 1152, 576
ROWS, LANES = 16, 128
NF, NPC = FEAT // ROWS, NP // LANES
CH = NF * NPC
AHEAD = 3
EXTRA = 2
NT = (((1,), (1,)), ((), ()))


def split3(v):
    hi = v.astype(BF16)
    rest = v - hi.astype(F32)
    mid = rest.astype(BF16)
    lo = (rest - mid.astype(F32)).astype(BF16)
    return jnp.concatenate([hi, mid, lo], axis=0)


def sum3(v):
    n = v.shape[0] // 3
    return (v[2 * n :] + v[n : 2 * n]) + v[:n]


def row_ones(r, width, value, dtype):
    rows = lax.broadcasted_iota(jnp.int32, (8, width), 0)
    return jnp.where(rows == r, F32(value), F32(0.0)).astype(dtype)


def kernel(*refs):
    (patches, picked_in, text, w_in, w_out, scale_in, bias_in, out) = refs[:8]
    refs = refs[8:]
    picked, scale_ref, bias_ref, send_idx, comp_idx, half_idx, pv, tv, ys, zs, xb, wb, tb, normed, acc, pooled, mean_rows, f1, f2, itl = refs[:20]
    yr = refs[20 : 20 + CH]
    zr = refs[20 + CH : 20 + 2 * CH]
    (lsem, ysend, yrecv, zsend, zrecv, zxsend, zxrecv, xsend, xrecv, wsend, wrecv, dsend, drecv,
     tsend, trecv, f1send, f1recv, f2send, f2recv) = refs[20 + 2 * CH :]

    dp = lax.axis_index("dp")
    mp = lax.axis_index("mp")
    y, h, c = dp // 4, (dp // 2) % 2, dp % 2
    q, x = mp // NX, mp % NX
    z = h * NQ + q
    me = y * NC + c
    yp = (y % 4) * 2 + y // 4

    def ydev(s):
        return (((s // 2) * 2 + h) * 2 + s % 2, mp)

    def zdev(t):
        return ((y * 2 + t // NQ) * 2 + c, (t % NQ) * NX + x)

    def xdev(k):
        return (dp, q * NX + k)

    def core_dev():
        return (y * 4 + h * 2 + 1 - c, mp)

    def remote(src, dst, ssem, rsem, dev):
        return pltpu.make_async_remote_copy(
            src_ref=src, dst_ref=dst, send_sem=ssem, recv_sem=rsem, device_id=dev, device_id_type=MESH)

    def wait(ref, sem):
        pltpu.make_async_copy(ref, ref, sem).wait()

    def load(i, src, dst):
        copy = pltpu.make_async_copy(src, dst, lsem.at[i])
        copy.start()
        return copy

    load_k = load(0, picked_in, picked)
    load_p = load(1, patches, pv)
    load_i = load(2, w_in, wb.at[0, q])
    load_o = load(3, w_out, wb.at[1, q])
    load_t = load(4, text, tv)
    load_s = load(5, scale_in, scale_ref)
    load_b = load(6, bias_in, bias_ref)

    barrier = pltpu.get_barrier_semaphore()

    def greet(dev):
        pl.semaphore_signal(barrier, inc=1, device_id=dev, device_id_type=MESH)

    @pl.loop(1, NS)
    def _(o):
        greet(ydev((me + o) % NS))

    @pl.loop(1, NZ)
    def _(o):
        greet(zdev((z + o) % NZ))

    @pl.loop(1, NX)
    def _(o):
        greet(xdev((x + o) % NX))

    def source_of(v):
        return (v * 4033) >> 19

    base = dp * SUP

    load_k.wait()

    @pl.loop(0, 32)
    def _(n):
        first, second = jnp.int32(0), jnp.int32(0)
        for i in reversed(range(IMG)):
            at = picked[n * IMG + i] - base
            mine = (at >= 0) & (at < SUP)
            second = jnp.where(mine, first, second)
            first = jnp.where(mine, at, first)
        to = (n // 4) * 8 + (n % 2) * 4 + ((n // 2) % 2) * 2
        send_idx[to] = first
        send_idx[to + 1] = second

    def far_first(o, n):
        away = n // 2 - (o + 1) // 2
        return (away * (1 - 2 * (o % 2)) + n) % n

    def gather(k):
        pc, fc = k // NF, k % NF

        @pl.loop(0, NS * 4, unroll=8)
        def _(s):
            image = pv[send_idx[s], fc * ROWS : (fc + 1) * ROWS, pc * LANES : (pc + 1) * LANES]
            ys[k, s // 4, s % 4] = image

        yr[k][pl.ds(me * 4, 4)] = ys[k, me]

    def start_y(k):
        def send(s):
            remote(ys.at[k, s], yr[k].at[pl.ds(me * 4, 4)], ysend.at[k], yrecv.at[k], ydev(s)).start()

        @pl.loop(0, NY - 1)
        def _(o):
            to = (y + far_first(o, NY)) % NY
            send(to * 2 + c)
            send(to * 2 + 1 - c)

        send(me + 1 - 2 * c)

    load_p.wait()
    gather(0)
    pl.semaphore_wait(barrier, NS - 1 + NZ - 1 + NX - 1)
    start_y(0)
    up, down = (z + 1) % NZ, (z + NZ - 1) % NZ

    def qq(k):
        return (q + k + NQ) % NQ

    def w_piece(rnd, way):
        k = qq(-rnd if way == 0 else rnd)
        if rnd == 2:
            return wb.at[c, k, pl.ds(0 if way == 0 else 48, 48)]
        return wb.at[c, k]

    def w_copy(rnd, way):
        piece = w_piece(rnd, way)
        return remote(piece, piece, wsend.at[rnd, way], wrecv.at[rnd, way], zdev(up if way == 0 else down))

    def w_start(rnd):
        w_copy(rnd, 0).start()
        w_copy(rnd, 1).start()

    def w_wait(rnd):
        w_copy(rnd, 0).wait_recv()
        w_copy(rnd, 1).wait_recv()

    def d_copy(j):
        k = (qq(-1), qq(1), qq(-2), qq(2), qq(3))[j]
        return remote(wb.at[c, k], wb.at[c, k], dsend.at[j], drecv.at[j], core_dev())

    gather(1)
    start_y(1)
    load_i.wait()
    load_o.wait()
    w_start(0)
    for k in range(2, AHEAD):
        gather(k)
        start_y(k)

    for e in range(NH):
        sources = []
        for i in range(IMG):
            source = source_of(picked[((y * NH + e) * NC + c) * IMG + i])
            slot = jnp.int32(0)
            for other in sources:
                slot = jnp.where(other == source, 1, slot)
            sources.append(source)
            block = (source // 4) * 8 + (source % 2) * 4 + e * 2 + slot
            to = (e * NQ * 2 + i) if i < IMG - 1 else NZ * 2 + e
            comp_idx[to] = jnp.where((source // 2) % 2 == h, block, 0)
    for r in range(3):
        source = source_of(picked[dp * IMG + (2 * q + r if r < 2 else IMG - 1)])
        half_idx[r] = ((source // 2) % 2) * NQ

    load_t.wait()
    load_s.wait()
    load_b.wait()

    @pl.when(y % 4 == x)
    def _():
        tb[c, h, yp] = jnp.concatenate([tv[...].astype(F32), jnp.zeros((ROWS - IMG, D), F32)], axis=0).astype(BF16)

    def t_spread():
        @pl.when(y % 4 == x)
        def _():
            @pl.loop(0, NY - 1)
            def _(o):
                to = (y + far_first(o, NY)) % NY
                remote(tb.at[c, h, yp], tb.at[c, h, yp], tsend.at[0], trecv.at[y // 4], ((to * 2 + h) * 2 + c, mp)).start()

    def t_mirror():
        piece = tb.at[c, h, pl.ds(2 * x, 2)]
        return remote(piece, piece, tsend.at[1], trecv.at[2], zdev(NZ - 1 - z))

    def t_gather(k):
        piece = tb.at[c, :, pl.ds(2 * x, 2)]
        return remote(piece, piece, tsend.at[2], trecv.at[3 + x], xdev(k))

    def t_core():
        return remote(tb.at[c], tb.at[c], tsend.at[3], trecv.at[7], core_dev())

    def compact(k):
        @pl.loop(0, NZ * 2 + NH, unroll=13)
        def _(g):
            zs[k, g] = yr[k][comp_idx[g]]

        zr[k][z, 0:2] = zs[k, pl.ds(2 * z, 2)]
        zr[k][z, 2] = zs[k, NZ * 2 + h]

    def start_z(k):
        @pl.loop(0, NZ - 1)
        def _(o):
            t = (z + far_first(o, NZ)) % NZ
            remote(zs.at[k, pl.ds(2 * t, 2)], zr[k].at[z, pl.ds(0, 2)], zsend.at[k], zrecv.at[k], zdev(t)).start()

        for e in range(NH):
            t = e * NQ + EXTRA

            @pl.when(z != t)
            def _():
                remote(zs.at[k, pl.ds(NZ * 2 + e, 1)], zr[k].at[z, pl.ds(2, 1)], zxsend.at[k, e], zxrecv.at[k], zdev(t)).start()

    extra = q == EXTRA

    def wait_z(k):
        wait(zr[k].at[pl.ds(0, NZ - 1), pl.ds(0, 2)], zrecv.at[k])

        @pl.when(extra)
        def _():
            wait(zr[k].at[pl.ds(0, NZ - 1), pl.ds(2, 1)], zxrecv.at[k])

    def select(k):
        pc, fc = k // NF, k % NF

        @pl.loop(0, NQ)
        def _(s):
            for r in range(2):
                xb[pc, r, s, x, fc] = zr[k][half_idx[r] + s, r]

        @pl.when(extra)
        def _():
            @pl.loop(0, NQ)
            def _(s):
                xb[pc, 2, s, x, fc] = zr[k][half_idx[2] + s, 2]

    def x_piece(k, r0, n, owner):
        return xb.at[k // NF, pl.ds(r0, n), :, owner, k % NF]

    def x_copy(k, r0, n, owner, to):
        piece = x_piece(k, r0, n, owner)
        i = 0 if r0 == 0 else 1
        return remote(piece, piece, xsend.at[k, i, to], xrecv.at[k, i, owner], xdev(to))

    def start_x(k):
        @pl.loop(1, NX)
        def _(o):
            x_copy(k, 0, 2, x, (x + o) % NX).start()

        @pl.when(extra)
        def _():
            @pl.loop(1, NX)
            def _(o):
                x_copy(k, 2, 1, x, (x + o) % NX).start()

    def wait_x(k):
        @pl.loop(1, NX)
        def _(o):
            owner = (x + o) % NX
            wait(x_piece(k, 0, 2, owner), xrecv.at[k, 0, owner])

        @pl.when(extra)
        def _():
            @pl.loop(1, NX)
            def _(o):
                owner = (x + o) % NX
                wait(x_piece(k, 2, 1, owner), xrecv.at[k, 1, owner])

    def normalize(pc, r):
        flat = xb[pc, r].reshape(D, LANES)
        values = flat.astype(F32)
        center = jnp.sum(values, axis=0, keepdims=True) * F32(1.0 / D)
        values = values - center
        spread = jnp.sum(values * values, axis=0, keepdims=True) * F32(1.0 / D)
        mean = lax.dot_general(row_ones(r, LANES, 1.0 / (NP * NX), BF16), flat, NT, preferred_element_type=F32)
        mean_rows[...] += mean
        return (values * lax.rsqrt(spread + F32(EPS))).astype(BF16)

    def hidden(pc, lanes, first):
        weights = wb[0].reshape(HID, D)
        value = jnp.dot(weights, normed[:, lanes], preferred_element_type=F32)
        value = jax.nn.gelu(value, approximate=True)
        if pc == 0:
            acc[:, lanes] = value
        else:
            acc[:, lanes] += value

    def compute(pc):
        normed[:, 0:LANES] = normalize(pc, 0)
        normed[:, LANES : 2 * LANES] = normalize(pc, 1)
        hidden(pc, slice(0, 2 * LANES), 0)

        @pl.when(extra)
        def _():
            normed[:, 2 * LANES :] = normalize(pc, 2)
            hidden(pc, slice(2 * LANES, 3 * LANES), 2)

    def pool(r):
        total = acc[:, r * LANES : (r + 1) * LANES]
        pooled[...] += lax.dot_general(
            row_ones(r, LANES, 1.0 / NP, F32), total, NT, precision=lax.Precision.HIGHEST, preferred_element_type=F32)

    mean_rows[...] = jnp.zeros((8, D), F32)
    pooled[...] = jnp.zeros((8, HID), F32)

    for k in range(CH):
        wait(yr[k].at[pl.ds(0, (NS - 1) * 4)], yrecv.at[k])
        compact(k)
        start_z(k)
        if k == 1:
            w_wait(0)
            w_start(1)
            d_copy(0).start()
            d_copy(1).start()
        elif k == 2:
            w_wait(1)
            w_start(2)
            d_copy(2).start()
            d_copy(3).start()
        elif k == 3:
            w_wait(2)
            d_copy(4).start()
        if k + AHEAD < CH:
            gather(k + AHEAD)
            start_y(k + AHEAD)
        if k + AHEAD == CH - 1:
            t_spread()
        if k >= 1:
            wait_z(k - 1)
            select(k - 1)
            start_x(k - 1)
    for j in range(2):

        @pl.when(2 * x + j != yp)
        def _():
            wait(tb.at[c, h, 2 * x + j], trecv.at[j])

    t_mirror().start()
    for j in range(5):
        kk = (qq(-1), qq(1), qq(-2), qq(2), qq(3))[j]
        wait(wb.at[1 - c, kk], drecv.at[j])
    for j in range(NF):
        wait_x(j)
    compute(0)
    wait_z(CH - 1)
    select(CH - 1)
    start_x(CH - 1)
    t_mirror().wait_recv()

    @pl.loop(1, NX)
    def _(o):
        t_gather((x + o) % NX).start()

    for j in range(NF, CH):
        wait_x(j)
    compute(1)
    pool(0)
    pool(1)

    @pl.when(extra)
    def _():
        pool(2)

    embed = jnp.dot(pooled[...].astype(BF16), wb[1].reshape(HID, D), preferred_element_type=F32)
    embed = embed + mean_rows[...]
    for r in range(3):
        f1[x, r] = embed[r : r + 1]

    def by_rows(step):
        @pl.when(extra)
        def _():
            step(3)

        @pl.when(q != EXTRA)
        def _():
            step(2)

    def f1_copy(n, to):
        rows = f1.at[x, pl.ds(0, n)]
        return remote(rows, rows, f1send.at[to], f1recv.at[x], xdev(to))

    def f2_copy(n, to):
        rows = f2.at[q, pl.ds(0, n)]
        return remote(rows, rows, f2send.at[to], f2recv.at[q], (dp, to * NX + x))

    @by_rows
    def _(n):
        @pl.loop(1, NX)
        def _(o):
            f1_copy(n, (x + o) % NX).start()

        @pl.loop(1, NX)
        def _(o):
            owner = (x + o) % NX
            wait(tb.at[c, :, pl.ds(2 * owner, 2)], trecv.at[3 + owner])

        t_core().start()

        @pl.loop(1, NX)
        def _(o):
            owner = (x + o) % NX
            wait(f1.at[owner, pl.ds(0, n)], f1recv.at[owner])

        rows = slice(0, n)
        f2[q, rows] = (f1[0, rows] + f1[1, rows]) + (f1[2, rows] + f1[3, rows])

        @pl.loop(1, NQ)
        def _(o):
            f2_copy(n, (q + o) % NQ).start()

    wait(tb.at[1 - c], trecv.at[7])
    squares = tb[...].reshape(NS * NH * ROWS, D).astype(F32)
    squares = squares * squares
    hi = squares.astype(BF16)
    lo = (squares - hi.astype(F32)).astype(BF16)
    ones = jnp.ones((8, D), BF16)
    total = lax.dot_general(ones, lo, NT, preferred_element_type=F32)
    total = total + lax.dot_general(ones, hi, NT, preferred_element_type=F32)
    itl[...] = 1.0 / jnp.sqrt(total + F32(EPS))

    for owner in range(NQ):

        @pl.when(owner != q)
        def _():
            wait(f2.at[owner, pl.ds(0, 3 if owner == EXTRA else 2)], f2recv.at[owner])

    embed = jnp.concatenate(
        [f2[k, r] for k in range(NQ) for r in range(2)] + [f2[EXTRA, 2], jnp.zeros((ROWS - IMG, D), F32)], axis=0)
    length = jnp.sqrt(jnp.sum(embed * embed, axis=1, keepdims=True) + F32(EPS))
    unit = embed / length
    scale = scale_ref[0]
    table = tb[...].reshape(NS * NH * ROWS, D)
    dots = sum3(lax.dot_general(split3(unit), table, NT, preferred_element_type=F32))
    inverse = itl[0:1, :]
    logits = scale * (dots * inverse) + bias_ref[0]
    row = lax.broadcasted_iota(jnp.int32, logits.shape, 0)
    col = lax.broadcasted_iota(jnp.int32, logits.shape, 1)
    label = jnp.where(col == ((c * NH + h) * NY + yp) * ROWS + row, F32(1.0), F32(-1.0))
    slope = -label * jax.nn.sigmoid(-label * logits)
    summed = sum3(jnp.dot(split3(slope * inverse), table, preferred_element_type=F32))
    unit_grad = scale * summed
    along = jnp.sum(unit * unit_grad, axis=1, keepdims=True)
    out[...] = ((unit_grad - unit * along) / length)[0:IMG]

    for k in range(CH):
        wait(yr[k].at[pl.ds(0, (NS - 1) * 4)], ysend.at[k])
        wait(zs.at[k, pl.ds(0, (NZ - 1) * 2)], zsend.at[k])
        for e in range(NH):
            t = e * NQ + EXTRA

            @pl.when(z != t)
            def _():
                wait(zs.at[k, pl.ds(NZ * 2 + e, 1)], zxsend.at[k, e])

        @pl.loop(1, NX)
        def _(o):
            x_copy(k, 0, 2, x, (x + o) % NX).wait_send()

        @pl.when(extra)
        def _():
            @pl.loop(1, NX)
            def _(o):
                x_copy(k, 2, 1, x, (x + o) % NX).wait_send()

    for rnd in range(3):
        w_copy(rnd, 0).wait_send()
        w_copy(rnd, 1).wait_send()
    for j in range(5):
        d_copy(j).wait_send()

    @pl.when(y % 4 == x)
    def _():
        wait(tb.at[c, h, pl.ds(0, NY - 1)], tsend.at[0])

    t_mirror().wait_send()
    wait(tb.at[pl.ds(0, 1), :, pl.ds(0, 6)], tsend.at[2])
    t_core().wait_send()

    @by_rows
    def _(n):
        @pl.loop(1, NX)
        def _(o):
            f1_copy(n, (x + o) % NX).wait_send()

        @pl.loop(1, NQ)
        def _(o):
            f2_copy(n, (q + o) % NQ).wait_send()


def body(patches, picked, text_embed, weight_in, weight_out, logit_scale, logit_bias):
    hbm = pl.BlockSpec(memory_space=pltpu.HBM)
    vmem = pl.BlockSpec(memory_space=pltpu.VMEM)
    dma = pltpu.SemaphoreType.DMA
    return pl.pallas_call(
        kernel,
        out_shape=jax.ShapeDtypeStruct((IMG, D), F32),
        in_specs=[hbm] * 7,
        out_specs=vmem,
        scratch_shapes=[
            pltpu.SMEM((32 * IMG,), jnp.int32),
            pltpu.SMEM((1,), F32),
            pltpu.SMEM((1,), F32),
            pltpu.SMEM((NS * 4,), jnp.int32),
            pltpu.SMEM((NZ * 2 + NH,), jnp.int32),
            pltpu.SMEM((3,), jnp.int32),
            pltpu.VMEM((SUP, FEAT, NP), BF16),
            pltpu.VMEM((IMG, D), BF16),
            pltpu.VMEM((CH, NS, 4, ROWS, LANES), BF16),
            pltpu.VMEM((CH, NZ * 2 + NH, ROWS, LANES), BF16),
            pltpu.VMEM((NPC, 3, NQ, NX, NF, ROWS, LANES), BF16),
            pltpu.VMEM((2, NQ, 96, D), BF16),
            pltpu.VMEM((NC, NH, NY, ROWS, D), BF16),
            pltpu.VMEM((D, 3 * LANES), BF16),
            pltpu.VMEM((HID, 3 * LANES), F32),
            pltpu.VMEM((8, HID), F32),
            pltpu.VMEM((8, D), F32),
            pltpu.VMEM((NX, 3, 1, D), F32),
            pltpu.VMEM((NQ, 3, 1, D), F32),
            pltpu.VMEM((8, NS * NH * ROWS), F32),
        ]
        + [pltpu.VMEM((NS * 4, ROWS, LANES), BF16)] * CH
        + [pltpu.VMEM((NZ, 3, ROWS, LANES), BF16)] * CH
        + [
            dma((7,)), dma((CH,)), dma((CH,)), dma((CH,)), dma((CH,)), dma((CH, NH)), dma((CH,)),
            dma((CH, 2, NX)), dma((CH, 2, NX)), dma((3, 2)), dma((3, 2)), dma((5,)), dma((5,)),
            dma((4,)), dma((8,)), dma((NX,)), dma((NX,)), dma((NQ,)), dma((NQ,)),
        ],
        compiler_params=pltpu.CompilerParams(
            collective_id=0, has_side_effects=True, vmem_limit_bytes=62 * 1024 * 1024),
        cost_estimate=pl.CostEstimate(flops=2_000_000_000, bytes_accessed=5_000_000, transcendentals=1_000_000),
    )(patches, picked, text_embed, weight_in.T, weight_out, logit_scale, logit_bias)


def solution(mesh):
    in_specs = (P("dp", "mp", None), P(), P("dp", None), P(None, "mp"), P("mp", None), P(), P())
    return jax.shard_map(body, mesh=mesh, in_specs=in_specs, out_specs=P("dp", None), check_vma=False)
```

```python
import jax
import jax.numpy as jnp
from jax import lax
from jax.experimental import pallas as pl
from jax.experimental.pallas import tpu as pltpu
from jax.sharding import PartitionSpec as P

MESH = pl.DeviceIdType.MESH
F32, BF16 = jnp.float32, jnp.bfloat16
EPS = 1e-06
NY, NH, NC, NQ, NX = 8, 2, 2, 6, 4
NZ = NH * NQ
NS = NY * NC
IMG = 13
SUP = 130
FEAT, NP = 48, 256
D, HID = 1152, 576
ROWS, LANES = 16, 128
NF, NPC = FEAT // ROWS, NP // LANES
CH = NF * NPC
AHEAD = 3
EXTRA = 2
NT = (((1,), (1,)), ((), ()))


def split3(v):
    hi = v.astype(BF16)
    rest = v - hi.astype(F32)
    mid = rest.astype(BF16)
    lo = (rest - mid.astype(F32)).astype(BF16)
    return jnp.concatenate([hi, mid, lo], axis=0)


def sum3(v):
    n = v.shape[0] // 3
    return (v[2 * n :] + v[n : 2 * n]) + v[:n]


def row_ones(r, width, value, dtype):
    rows = lax.broadcasted_iota(jnp.int32, (8, width), 0)
    return jnp.where(rows == r, F32(value), F32(0.0)).astype(dtype)


def kernel(*refs):
    (patches, picked_in, text, w_in, w_out, scale_in, bias_in, out) = refs[:8]
    refs = refs[8:]
    picked, scale_ref, bias_ref, send_idx, comp_idx, half_idx, pv, tv, ys, zs, xb, wb, tb, normed, acc, pooled, mean_rows, f1, f2, itl = refs[:20]
    yr = refs[20 : 20 + CH]
    zr = refs[20 + CH : 20 + 2 * CH]
    (lsem, ysend, yrecv, zsend, zrecv, zxsend, zxrecv, xsend, xrecv, wsend, wrecv, dsend, drecv,
     tsend, trecv, f1send, f1recv, f2send, f2recv) = refs[20 + 2 * CH :]

    dp = lax.axis_index("dp")
    mp = lax.axis_index("mp")
    y, h, c = dp // 4, (dp // 2) % 2, dp % 2
    q, x = mp // NX, mp % NX
    z = h * NQ + q
    me = y * NC + c
    yp = (y % 4) * 2 + y // 4

    def ydev(s):
        return (((s // 2) * 2 + h) * 2 + s % 2, mp)

    def zdev(t):
        return ((y * 2 + t // NQ) * 2 + c, (t % NQ) * NX + x)

    def xdev(k):
        return (dp, q * NX + k)

    def core_dev():
        return (y * 4 + h * 2 + 1 - c, mp)

    def remote(src, dst, ssem, rsem, dev):
        return pltpu.make_async_remote_copy(
            src_ref=src, dst_ref=dst, send_sem=ssem, recv_sem=rsem, device_id=dev, device_id_type=MESH)

    def wait(ref, sem):
        pltpu.make_async_copy(ref, ref, sem).wait()

    def load(i, src, dst):
        copy = pltpu.make_async_copy(src, dst, lsem.at[i])
        copy.start()
        return copy

    load_k = load(0, picked_in, picked)
    load_p = load(1, patches, pv)
    load_i = load(2, w_in, wb.at[0, q])
    load_o = load(3, w_out, wb.at[1, q])
    load_t = load(4, text, tv)
    load_s = load(5, scale_in, scale_ref)
    load_b = load(6, bias_in, bias_ref)

    barrier = pltpu.get_barrier_semaphore()

    def greet(dev):
        pl.semaphore_signal(barrier, inc=1, device_id=dev, device_id_type=MESH)

    @pl.loop(1, NS)
    def _(o):
        greet(ydev((me + o) % NS))

    @pl.loop(1, NZ)
    def _(o):
        greet(zdev((z + o) % NZ))

    @pl.loop(1, NX)
    def _(o):
        greet(xdev((x + o) % NX))

    def source_of(v):
        return (v * 4033) >> 19

    base = dp * SUP

    load_k.wait()

    @pl.loop(0, 32)
    def _(n):
        first, second = jnp.int32(0), jnp.int32(0)
        for i in reversed(range(IMG)):
            at = picked[n * IMG + i] - base
            mine = (at >= 0) & (at < SUP)
            second = jnp.where(mine, first, second)
            first = jnp.where(mine, at, first)
        to = (n // 4) * 8 + (n % 2) * 4 + ((n // 2) % 2) * 2
        send_idx[to] = first
        send_idx[to + 1] = second

    def far_first(o, n):
        away = n // 2 - (o + 1) // 2
        return (away * (1 - 2 * (o % 2)) + n) % n

    def gather(k):
        pc, fc = k // NF, k % NF

        @pl.loop(0, NS * 4, unroll=8)
        def _(s):
            image = pv[send_idx[s], fc * ROWS : (fc + 1) * ROWS, pc * LANES : (pc + 1) * LANES]
            ys[k, s // 4, s % 4] = image

        yr[k][pl.ds(me * 4, 4)] = ys[k, me]

    def start_y(k):
        def send(s):
            remote(ys.at[k, s], yr[k].at[pl.ds(me * 4, 4)], ysend.at[k], yrecv.at[k], ydev(s)).start()

        @pl.loop(0, NY - 1)
        def _(o):
            to = (y + far_first(o, NY)) % NY
            send(to * 2 + c)
            send(to * 2 + 1 - c)

        send(me + 1 - 2 * c)

    up, down = (z + 1) % NZ, (z + NZ - 1) % NZ

    def qq(k):
        return (q + k + NQ) % NQ

    def w_piece(rnd, way):
        k = qq(-rnd if way == 0 else rnd)
        if rnd == 2:
            return wb.at[c, k, pl.ds(0 if way == 0 else 48, 48)]
        return wb.at[c, k]

    def w_copy(rnd, way):
        piece = w_piece(rnd, way)
        return remote(piece, piece, wsend.at[rnd, way], wrecv.at[rnd, way], zdev(up if way == 0 else down))

    def w_start(rnd):
        w_copy(rnd, 0).start()
        w_copy(rnd, 1).start()

    def w_wait(rnd):
        w_copy(rnd, 0).wait_recv()
        w_copy(rnd, 1).wait_recv()

    def d_copy(j):
        k = (qq(-1), qq(1), qq(-2), qq(2), qq(3))[j]
        return remote(wb.at[c, k], wb.at[c, k], dsend.at[j], drecv.at[j], core_dev())

    load_p.wait()
    gather(0)
    pl.semaphore_wait(barrier, NS - 1 + NZ - 1 + NX - 1)
    load_i.wait()
    load_o.wait()
    w_start(0)
    start_y(0)
    gather(1)
    start_y(1)
    for k in range(2, AHEAD):
        gather(k)
        start_y(k)

    for e in range(NH):
        sources = []
        for i in range(IMG):
            source = source_of(picked[((y * NH + e) * NC + c) * IMG + i])
            slot = jnp.int32(0)
            for other in sources:
                slot = jnp.where(other == source, 1, slot)
            sources.append(source)
            block = (source // 4) * 8 + (source % 2) * 4 + e * 2 + slot
            to = (e * NQ * 2 + i) if i < IMG - 1 else NZ * 2 + e
            comp_idx[to] = jnp.where((source // 2) % 2 == h, block, 0)
    for r in range(3):
        source = source_of(picked[dp * IMG + (2 * q + r if r < 2 else IMG - 1)])
        half_idx[r] = ((source // 2) % 2) * NQ

    load_t.wait()
    load_s.wait()
    load_b.wait()

    @pl.when(y % 4 == x)
    def _():
        tb[c, h, yp] = jnp.concatenate([tv[...].astype(F32), jnp.zeros((ROWS - IMG, D), F32)], axis=0).astype(BF16)

    def t_spread():
        @pl.when(y % 4 == x)
        def _():
            @pl.loop(0, NY - 1)
            def _(o):
                to = (y + far_first(o, NY)) % NY
                remote(tb.at[c, h, yp], tb.at[c, h, yp], tsend.at[0], trecv.at[y // 4], ((to * 2 + h) * 2 + c, mp)).start()

    def t_mirror():
        piece = tb.at[c, h, pl.ds(2 * x, 2)]
        return remote(piece, piece, tsend.at[1], trecv.at[2], zdev(NZ - 1 - z))

    def t_gather(k):
        piece = tb.at[c, :, pl.ds(2 * x, 2)]
        return remote(piece, piece, tsend.at[2], trecv.at[3 + x], xdev(k))

    def t_core():
        return remote(tb.at[c], tb.at[c], tsend.at[3], trecv.at[7], core_dev())

    def compact(k):
        @pl.loop(0, NZ * 2 + NH, unroll=13)
        def _(g):
            zs[k, g] = yr[k][comp_idx[g]]

        zr[k][z, 0:2] = zs[k, pl.ds(2 * z, 2)]
        zr[k][z, 2] = zs[k, NZ * 2 + h]

    def start_z(k):
        @pl.loop(0, NZ - 1)
        def _(o):
            t = (z + far_first(o, NZ)) % NZ
            remote(zs.at[k, pl.ds(2 * t, 2)], zr[k].at[z, pl.ds(0, 2)], zsend.at[k], zrecv.at[k], zdev(t)).start()

        for e in range(NH):
            t = e * NQ + EXTRA

            @pl.when(z != t)
            def _():
                remote(zs.at[k, pl.ds(NZ * 2 + e, 1)], zr[k].at[z, pl.ds(2, 1)], zxsend.at[k, e], zxrecv.at[k], zdev(t)).start()

    extra = q == EXTRA

    def wait_z(k):
        wait(zr[k].at[pl.ds(0, NZ - 1), pl.ds(0, 2)], zrecv.at[k])

        @pl.when(extra)
        def _():
            wait(zr[k].at[pl.ds(0, NZ - 1), pl.ds(2, 1)], zxrecv.at[k])

    def select(k):
        pc, fc = k // NF, k % NF

        @pl.loop(0, NQ)
        def _(s):
            for r in range(2):
                xb[pc, r, s, x, fc] = zr[k][half_idx[r] + s, r]

        @pl.when(extra)
        def _():
            @pl.loop(0, NQ)
            def _(s):
                xb[pc, 2, s, x, fc] = zr[k][half_idx[2] + s, 2]

    def x_piece(k, r0, n, owner):
        return xb.at[k // NF, pl.ds(r0, n), :, owner, k % NF]

    def x_copy(k, r0, n, owner, to):
        piece = x_piece(k, r0, n, owner)
        i = 0 if r0 == 0 else 1
        return remote(piece, piece, xsend.at[k, i, to], xrecv.at[k, i, owner], xdev(to))

    def start_x(k):
        @pl.loop(1, NX)
        def _(o):
            x_copy(k, 0, 2, x, (x + o) % NX).start()

        @pl.when(extra)
        def _():
            @pl.loop(1, NX)
            def _(o):
                x_copy(k, 2, 1, x, (x + o) % NX).start()

    def wait_x(k):
        @pl.loop(1, NX)
        def _(o):
            owner = (x + o) % NX
            wait(x_piece(k, 0, 2, owner), xrecv.at[k, 0, owner])

        @pl.when(extra)
        def _():
            @pl.loop(1, NX)
            def _(o):
                owner = (x + o) % NX
                wait(x_piece(k, 2, 1, owner), xrecv.at[k, 1, owner])

    def normalize(pc, r):
        flat = xb[pc, r].reshape(D, LANES)
        values = flat.astype(F32)
        center = jnp.sum(values, axis=0, keepdims=True) * F32(1.0 / D)
        values = values - center
        spread = jnp.sum(values * values, axis=0, keepdims=True) * F32(1.0 / D)
        mean = lax.dot_general(row_ones(r, LANES, 1.0 / (NP * NX), BF16), flat, NT, preferred_element_type=F32)
        mean_rows[...] += mean
        return (values * lax.rsqrt(spread + F32(EPS))).astype(BF16)

    def hidden(pc, lanes, first):
        weights = wb[0].reshape(HID, D)
        value = jnp.dot(weights, normed[:, lanes], preferred_element_type=F32)
        value = jax.nn.gelu(value, approximate=True)
        if pc == 0:
            acc[:, lanes] = value
        else:
            acc[:, lanes] += value

    def compute(pc):
        normed[:, 0:LANES] = normalize(pc, 0)
        normed[:, LANES : 2 * LANES] = normalize(pc, 1)
        hidden(pc, slice(0, 2 * LANES), 0)

        @pl.when(extra)
        def _():
            normed[:, 2 * LANES :] = normalize(pc, 2)
            hidden(pc, slice(2 * LANES, 3 * LANES), 2)

    def pool(r):
        total = acc[:, r * LANES : (r + 1) * LANES]
        pooled[...] += lax.dot_general(
            row_ones(r, LANES, 1.0 / NP, F32), total, NT, precision=lax.Precision.HIGHEST, preferred_element_type=F32)

    mean_rows[...] = jnp.zeros((8, D), F32)
    pooled[...] = jnp.zeros((8, HID), F32)

    for k in range(CH):
        wait(yr[k].at[pl.ds(0, (NS - 1) * 4)], yrecv.at[k])
        compact(k)
        start_z(k)
        if k == 0:
            w_wait(0)
            w_start(1)
            d_copy(0).start()
            d_copy(1).start()
        elif k == 1:
            w_wait(1)
            w_start(2)
            d_copy(2).start()
            d_copy(3).start()
        elif k == 2:
            w_wait(2)
            d_copy(4).start()
        if k + AHEAD < CH:
            gather(k + AHEAD)
            start_y(k + AHEAD)
        if k + AHEAD == CH - 1:
            t_spread()
        if k >= 2:
            wait_z(k - 2)
            select(k - 2)
            start_x(k - 2)
    wait_z(CH - 2)
    select(CH - 2)
    start_x(CH - 2)
    for j in range(2):

        @pl.when(2 * x + j != yp)
        def _():
            wait(tb.at[c, h, 2 * x + j], trecv.at[j])

    t_mirror().start()
    for j in range(5):
        kk = (qq(-1), qq(1), qq(-2), qq(2), qq(3))[j]
        wait(wb.at[1 - c, kk], drecv.at[j])
    for j in range(NF):
        wait_x(j)
    compute(0)
    wait_z(CH - 1)
    select(CH - 1)
    start_x(CH - 1)
    t_mirror().wait_recv()

    @pl.loop(1, NX)
    def _(o):
        t_gather((x + o) % NX).start()

    for j in range(NF, CH):
        wait_x(j)
    compute(1)
    pool(0)
    pool(1)

    @pl.when(extra)
    def _():
        pool(2)

    embed = jnp.dot(pooled[...].astype(BF16), wb[1].reshape(HID, D), preferred_element_type=F32)
    embed = embed + mean_rows[...]
    for r in range(3):
        f1[x, r] = embed[r : r + 1]

    def by_rows(step):
        @pl.when(extra)
        def _():
            step(3)

        @pl.when(q != EXTRA)
        def _():
            step(2)

    def f1_copy(n, to):
        rows = f1.at[x, pl.ds(0, n)]
        return remote(rows, rows, f1send.at[to], f1recv.at[x], xdev(to))

    def f2_copy(n, to):
        rows = f2.at[q, pl.ds(0, n)]
        return remote(rows, rows, f2send.at[to], f2recv.at[q], (dp, to * NX + x))

    @by_rows
    def _(n):
        @pl.loop(1, NX)
        def _(o):
            f1_copy(n, (x + o) % NX).start()

        @pl.loop(1, NX)
        def _(o):
            owner = (x + o) % NX
            wait(f1.at[owner, pl.ds(0, n)], f1recv.at[owner])

        rows = slice(0, n)
        f2[q, rows] = (f1[0, rows] + f1[1, rows]) + (f1[2, rows] + f1[3, rows])

        @pl.loop(1, NQ)
        def _(o):
            f2_copy(n, (q + o) % NQ).start()

    @pl.loop(1, NX)
    def _(o):
        owner = (x + o) % NX
        wait(tb.at[c, :, pl.ds(2 * owner, 2)], trecv.at[3 + owner])

    t_core().start()

    def lengths(half):
        squares = tb[half].reshape(NS * ROWS, D).astype(F32)
        squares = squares * squares
        hi = squares.astype(BF16)
        lo = (squares - hi.astype(F32)).astype(BF16)
        ones = jnp.ones((8, D), BF16)
        total = lax.dot_general(ones, lo, NT, preferred_element_type=F32)
        total = total + lax.dot_general(ones, hi, NT, preferred_element_type=F32)
        itl[half] = 1.0 / jnp.sqrt(total + F32(EPS))

    lengths(c)
    wait(tb.at[1 - c], trecv.at[7])
    lengths(1 - c)

    for owner in range(NQ):

        @pl.when(owner != q)
        def _():
            wait(f2.at[owner, pl.ds(0, 3 if owner == EXTRA else 2)], f2recv.at[owner])

    embed = jnp.concatenate(
        [f2[k, r] for k in range(NQ) for r in range(2)] + [f2[EXTRA, 2], jnp.zeros((ROWS - IMG, D), F32)], axis=0)
    length = jnp.sqrt(jnp.sum(embed * embed, axis=1, keepdims=True) + F32(EPS))
    unit = embed / length
    scale = scale_ref[0]
    table = tb[...].reshape(NS * NH * ROWS, D)
    dots = sum3(lax.dot_general(split3(unit), table, NT, preferred_element_type=F32))
    inverse = jnp.concatenate([itl[0, 0:1], itl[1, 0:1]], axis=1)
    logits = scale * (dots * inverse) + bias_ref[0]
    row = lax.broadcasted_iota(jnp.int32, logits.shape, 0)
    col = lax.broadcasted_iota(jnp.int32, logits.shape, 1)
    label = jnp.where(col == ((c * NH + h) * NY + yp) * ROWS + row, F32(1.0), F32(-1.0))
    slope = -label * jax.nn.sigmoid(-label * logits)
    summed = sum3(jnp.dot(split3(slope * inverse), table, preferred_element_type=F32))
    unit_grad = scale * summed
    along = jnp.sum(unit * unit_grad, axis=1, keepdims=True)
    out[...] = ((unit_grad - unit * along) / length)[0:IMG]

    for k in range(CH):
        wait(yr[k].at[pl.ds(0, (NS - 1) * 4)], ysend.at[k])
        wait(zs.at[k, pl.ds(0, (NZ - 1) * 2)], zsend.at[k])
        for e in range(NH):
            t = e * NQ + EXTRA

            @pl.when(z != t)
            def _():
                wait(zs.at[k, pl.ds(NZ * 2 + e, 1)], zxsend.at[k, e])

        @pl.loop(1, NX)
        def _(o):
            x_copy(k, 0, 2, x, (x + o) % NX).wait_send()

        @pl.when(extra)
        def _():
            @pl.loop(1, NX)
            def _(o):
                x_copy(k, 2, 1, x, (x + o) % NX).wait_send()

    for rnd in range(3):
        w_copy(rnd, 0).wait_send()
        w_copy(rnd, 1).wait_send()
    for j in range(5):
        d_copy(j).wait_send()

    @pl.when(y % 4 == x)
    def _():
        wait(tb.at[c, h, pl.ds(0, NY - 1)], tsend.at[0])

    t_mirror().wait_send()
    wait(tb.at[pl.ds(0, 1), :, pl.ds(0, 6)], tsend.at[2])
    t_core().wait_send()

    @by_rows
    def _(n):
        @pl.loop(1, NX)
        def _(o):
            f1_copy(n, (x + o) % NX).wait_send()

        @pl.loop(1, NQ)
        def _(o):
            f2_copy(n, (q + o) % NQ).wait_send()


def body(patches, picked, text_embed, weight_in, weight_out, logit_scale, logit_bias):
    hbm = pl.BlockSpec(memory_space=pltpu.HBM)
    vmem = pl.BlockSpec(memory_space=pltpu.VMEM)
    dma = pltpu.SemaphoreType.DMA
    return pl.pallas_call(
        kernel,
        out_shape=jax.ShapeDtypeStruct((IMG, D), F32),
        in_specs=[hbm] * 7,
        out_specs=vmem,
        scratch_shapes=[
            pltpu.SMEM((32 * IMG,), jnp.int32),
            pltpu.SMEM((1,), F32),
            pltpu.SMEM((1,), F32),
            pltpu.SMEM((NS * 4,), jnp.int32),
            pltpu.SMEM((NZ * 2 + NH,), jnp.int32),
            pltpu.SMEM((3,), jnp.int32),
            pltpu.VMEM((SUP, FEAT, NP), BF16),
            pltpu.VMEM((IMG, D), BF16),
            pltpu.VMEM((CH, NS, 4, ROWS, LANES), BF16),
            pltpu.VMEM((CH, NZ * 2 + NH, ROWS, LANES), BF16),
            pltpu.VMEM((NPC, 3, NQ, NX, NF, ROWS, LANES), BF16),
            pltpu.VMEM((2, NQ, 96, D), BF16),
            pltpu.VMEM((NC, NH, NY, ROWS, D), BF16),
            pltpu.VMEM((D, 3 * LANES), BF16),
            pltpu.VMEM((HID, 3 * LANES), F32),
            pltpu.VMEM((8, HID), F32),
            pltpu.VMEM((8, D), F32),
            pltpu.VMEM((NX, 3, 1, D), F32),
            pltpu.VMEM((NQ, 3, 1, D), F32),
            pltpu.VMEM((NC, 8, NS * ROWS), F32),
        ]
        + [pltpu.VMEM((NS * 4, ROWS, LANES), BF16)] * CH
        + [pltpu.VMEM((NZ, 3, ROWS, LANES), BF16)] * CH
        + [
            dma((7,)), dma((CH,)), dma((CH,)), dma((CH,)), dma((CH,)), dma((CH, NH)), dma((CH,)),
            dma((CH, 2, NX)), dma((CH, 2, NX)), dma((3, 2)), dma((3, 2)), dma((5,)), dma((5,)),
            dma((4,)), dma((8,)), dma((NX,)), dma((NX,)), dma((NQ,)), dma((NQ,)),
        ],
        compiler_params=pltpu.CompilerParams(
            collective_id=0, has_side_effects=True, vmem_limit_bytes=55000 * 1024),
        cost_estimate=pl.CostEstimate(flops=2_000_000_000, bytes_accessed=5_000_000, transcendentals=1_000_000),
    )(patches, picked, text_embed, weight_in.T, weight_out, logit_scale, logit_bias)


def solution(mesh):
    in_specs = (P("dp", "mp", None), P(), P("dp", None), P(None, "mp"), P("mp", None), P(), P())
    return jax.shard_map(body, mesh=mesh, in_specs=in_specs, out_specs=P("dp", None), check_vma=False)
```
